512 devices in a mesh: panel: 32 (over x, y, core), tile: 16 (over z).
Axes of the slice: x: 4, y: 4, z: 16, core: 2. Of those that a mesh axis runs over, the one named last changes fastest.
Arguments:
- target: float32 [8192, 2048], P('tile', 'panel'), may hold values from -6 to 6
- left_factors: bfloat16 [96, 8192, 256], P('panel', 'tile'), may hold values from -0.375 to 0.375
- right_factors: bfloat16 [96, 4, 2048, 256], P('panel', None, 'tile'), may hold values from -0.125 to 0.125
- diag_left: bfloat16 [96, 2048, 256], P('panel', 'tile'), may hold values from -1.25 to 1.25
- diag_right: bfloat16 [96, 2048, 256], P('panel', 'tile'), may hold values from -0.125 to 0.125
- tile_ranks: int32 [96, 4], P('panel'), may hold values from 64 to 256
- diag_ranks: int32 [96], P('panel'), may hold values from 64 to 256
Outputs:
- updated: float32 [8192, 2048], P('tile', 'panel')
The draws below stay inside these ranges and needn't reach their ends.
All inputs are finite; a program needn't handle non-finite values.
Results may differ from the reference program's by a relative error of at most 0.0011.
Values may be sent and summed in bfloat16 or wider, within the bound.
No kernel may reach another device: no remote copies, remote signals or barrier semaphores. Data moves between devices by JAX's collectives and lax.ppermute only.
A program may use at most 64 MiB of HBM per device.

```python
import jax
import jax.numpy as jnp
from jax import lax

NB = 2048
R = 256
J = 96
ROWS = 8192
MT = 4
N_TILE = 16


def place_ends(entries, rng, low, high):
    index_at = [jax.random.randint(jax.random.fold_in(rng, axis), (), 0, length) for axis, length in enumerate(entries.shape)]
    widest = entries.shape.index(max(entries.shape))
    neighbour = index_at[:widest] + [(index_at[widest] + 1) % entries.shape[widest]] + index_at[widest + 1:]
    return entries.at[tuple(index_at)].set(low).at[tuple(neighbour)].set(high)


def spiked(values, key, source, target, shards_of, factor):
    def block_of(dim):
        return (jnp.arange(values.shape[dim]) // (values.shape[dim] // shards_of)).reshape((-1,) + (1,) * (values.ndim - 1 - dim))

    first = jax.random.permutation(key, shards_of)[block_of(target)]
    second = (block_of(target) + shards_of // 2) % shards_of
    return jnp.where((block_of(source) == first) | (block_of(source) == second), factor * values, values)


def shard_levels(stream_key, extent, pieces, low, high):
    loudness = 1.0
    for axis_at, blocks in pieces:
        draws = jax.random.uniform(jax.random.fold_in(jax.random.fold_in(stream_key, 6), axis_at), (blocks,), jnp.float32, low / len(pieces), high / len(pieces))
        loudness = loudness * jnp.repeat(jnp.exp(draws), extent[axis_at] // blocks).reshape((-1,) + (1,) * (len(extent) - 1 - axis_at))
    return loudness


def centred(own_key, dims, deviation, most, cuts=(), held_as=jnp.bfloat16):
    level = shard_levels(own_key, dims, cuts, -0.22, 0.18) if cuts else 1.0
    entries = jax.random.normal(own_key, dims, jnp.float32) * deviation * level
    return jnp.minimum(jnp.maximum(entries, -most), most).astype(held_as)


def bell_draw_with(key, extent, spread, most, cuts, heavy, kind=jnp.bfloat16):
    array = spread * jax.random.normal(key, extent, jnp.float32)
    if cuts:
        array = array * shard_levels(key, extent, cuts, -0.22, 0.18)
    return jnp.clip(spiked(array, jax.random.fold_in(key, 3), *heavy), -most, most).astype(kind)


def setup_inputs(seed: int = 0) -> dict:
    key_list = jax.random.split(jax.random.key(seed), 8)
    target = centred(key_list[0], (ROWS, NB), 1.0, 6.0, ((0, 16), (1, 32)), jnp.float32)
    left_factors = centred(key_list[1], (J, ROWS, R), R ** -0.5, 0.375, ((0, 32), (1, 16)))
    right_factors = centred(key_list[2], (J, MT, NB, R), NB ** -0.5, 0.125, ((0, 32), (2, 16)))
    diag_left = bell_draw_with(key_list[3], (J, NB, R), J ** -0.5, 1.25, ((0, 32), (1, 16)), (0, 1, 32, 2.75))
    diag_right = centred(key_list[4], (J, NB, R), NB ** -0.5, 0.125, ((0, 32), (1, 16)))
    tile_ranks = place_ends(jax.random.randint(key_list[5], (J, MT), R // 4, R + 1), jax.random.fold_in(key_list[5], 1), R // 4, R).astype(jnp.int32)
    diag_ranks = place_ends(jax.random.randint(key_list[6], (J,), R // 4, R + 1), jax.random.fold_in(key_list[6], 1), R // 4, R).astype(jnp.int32)
    return {"target": target, "left_factors": left_factors, "right_factors": right_factors, "diag_left": diag_left, "diag_right": diag_right, "tile_ranks": tile_ranks, "diag_ranks": diag_ranks}


def reference(target, left_factors, right_factors, diag_left, diag_right, tile_ranks, diag_ranks):
    positions = jnp.arange(R)

    def one_column(total, item):
        left, right, dleft, dright, tranks, drank = item
        product_pieces = right.reshape(MT, N_TILE, NB // N_TILE, R).astype(jnp.float32)
        diagonal_pieces = dright.reshape(N_TILE, NB // N_TILE, R).astype(jnp.float32)
        partial_product = jnp.einsum('liyu,iyk->liuk', product_pieces, diagonal_pieces)
        reduced_update = jnp.sum(partial_product, axis=1)
        keep = (positions[None, :, None] < tranks[:, None, None]) & (positions[None, None, :] < drank)
        core = jnp.where(keep, reduced_update, jnp.float32(0.0)).astype(jnp.bfloat16)
        rows = left.reshape(MT, NB, R).astype(jnp.float32)
        mixed = jnp.einsum('mnr,mrs->mns', rows, core.astype(jnp.float32)).astype(jnp.bfloat16)
        term = jnp.dot(mixed.reshape(ROWS, R), dleft.T, preferred_element_type=jnp.float32)
        return total + term, None

    start = jnp.zeros((ROWS, NB), jnp.float32)
    delta, _ = lax.scan(one_column, start, (left_factors, right_factors, diag_left, diag_right, tile_ranks, diag_ranks))
    return target - delta
```

```python
import jax
import jax.numpy as jnp
from jax import lax
from jax.sharding import PartitionSpec as P

CORES = 2
CORE_SCALE = 1024.0


def shards(target, left_factors, right_factors, diag_left, diag_right, tile_ranks, diag_ranks):
    column_count, row_dev, rank = left_factors.shape
    piece = diag_left.shape[1]
    tile_count = lax.axis_size("tile")
    panel_count = lax.axis_size("panel")
    chip_count = panel_count // CORES
    half = piece // CORES
    tile_size = piece * tile_count
    local_tile = lax.axis_index("tile") * row_dev // tile_size
    core_id = lax.axis_index("panel") % CORES
    swap = [(p, p ^ 1) for p in range(panel_count)]
    across = [[CORES * c + a for c in range(chip_count)] for a in range(CORES)]

    kept = lax.dynamic_slice_in_dim(diag_left, core_id * half, half, 1)
    given = lax.dynamic_slice_in_dim(diag_left, (1 - core_id) * half, half, 1)
    got = lax.ppermute(given, "panel", swap)
    diag_rows = lax.all_gather(jnp.concatenate([kept, got], 0), "tile", axis=1, tiled=True)

    partial_product = jnp.einsum(
        "jmcr,jcs->jmrs", right_factors, diag_right, preferred_element_type=jnp.float32
    )
    core_sum = lax.psum((partial_product * CORE_SCALE).astype(jnp.float16), "tile")
    mine = lax.dynamic_index_in_dim(core_sum, local_tile, 1, keepdims=False)
    mine = mine.astype(jnp.float32) * (1.0 / CORE_SCALE)
    tranks = lax.dynamic_index_in_dim(tile_ranks, local_tile, 1, keepdims=False)
    positions = jnp.arange(rank)
    keep = (positions[None, :, None] < tranks[:, None, None]) & (
        positions[None, None, :] < diag_ranks[:, None, None]
    )
    core = jnp.where(keep, mine, jnp.float32(0.0)).astype(jnp.bfloat16)
    mixed = jnp.einsum(
        "jnr,jrs->jns", left_factors, core, preferred_element_type=jnp.float32
    ).astype(jnp.bfloat16)
    both = jnp.concatenate([mixed, lax.ppermute(mixed, "panel", swap)], 0)

    terms = jnp.einsum("jcs,jns->cn", diag_rows, both, preferred_element_type=jnp.float32)
    terms = terms.astype(jnp.bfloat16).reshape(chip_count, half, row_dev)
    parts = lax.all_to_all(
        terms, "panel", split_axis=0, concat_axis=0, tiled=True, axis_index_groups=across
    )
    delta = jnp.sum(parts.astype(jnp.float32), axis=0)
    return target - delta.T


def solution(mesh):
    placed = (
        P("tile", "panel"),
        P("panel", "tile", None),
        P("panel", None, "tile", None),
        P("panel", "tile", None),
        P("panel", "tile", None),
        P("panel", None),
        P("panel"),
    )
    return jax.shard_map(
        shards, mesh=mesh, in_specs=placed, out_specs=P("tile", "panel"), check_vma=False
    )
```

```python
import functools

import jax
import jax.numpy as jnp
from jax import lax
from jax.experimental import pallas as pl
from jax.experimental.pallas import tpu as pltpu
from jax.sharding import PartitionSpec as P

CORES = 2
CORE_SCALE = 1024.0
GROUP = 8
VMEM_BYTES = 16 << 20


def mix(where, tranks, dranks, left, core, mixed):
    columns, _, rank = left.shape
    row = lax.broadcasted_iota(jnp.int32, (rank, rank), 0)
    col = lax.broadcasted_iota(jnp.int32, (rank, rank), 1)
    for j in range(columns):
        keep = (row < tranks[j, where[1]]) & (col < dranks[j])
        masked = jnp.where(keep, core[j].astype(jnp.float32), 0.0).astype(jnp.bfloat16)
        mixed[j] = lax.dot_general(
            masked, left[j], (((0,), (1,)), ((), ())), preferred_element_type=jnp.float32
        ).astype(jnp.bfloat16)


def expand(diag, mixed, out):
    columns, group, _, half, rank = diag.shape
    total = None
    for j in range(columns):
        part = jnp.dot(
            diag[j].reshape(group * half, rank), mixed[j], preferred_element_type=jnp.float32
        )
        total = part if total is None else total + part
    out[...] = total.reshape(out.shape).astype(out.dtype)


def give_kernel(where, tranks, dranks, left, core, diag, mixed, out):
    @pl.when(pl.program_id(0) == 0)
    def _():
        mix(where, tranks, dranks, left, core, mixed)

    expand(diag, mixed, out)


def keep_kernel(where, mixed, diag, out):
    expand(diag, mixed, out)


def whole(shape):
    return pl.BlockSpec(shape, lambda i, *_: (0,) * len(shape))


def shards(target, left_factors, right_factors, diag_left, diag_right, tile_ranks, diag_ranks):
    column_count, row_dev, rank = left_factors.shape
    piece = diag_left.shape[1]
    tile_count = lax.axis_size("tile")
    panel_count = lax.axis_size("panel")
    chip_count = panel_count // CORES
    half = piece // CORES
    tile_size = piece * tile_count
    local_tile = lax.axis_index("tile") * row_dev // tile_size
    core_id = lax.axis_index("panel") % CORES
    swap = [(p, p ^ 1) for p in range(panel_count)]
    across = [[CORES * c + a for c in range(chip_count)] for a in range(CORES)]

    diag_rows = lax.all_gather(diag_left, "tile", axis=1, tiled=True)
    diag_rows = diag_rows.reshape(column_count, tile_count, CORES, half, rank)

    partial_product = jnp.einsum(
        "jmcr,jcs->jmrs", right_factors, diag_right, preferred_element_type=jnp.float32
    )
    core_sum = lax.psum((partial_product * CORE_SCALE).astype(jnp.float16), "tile")
    mine = lax.dynamic_index_in_dim(core_sum, local_tile, 1, keepdims=False)
    core = (mine.astype(jnp.float32) * (1.0 / CORE_SCALE)).astype(jnp.bfloat16)

    where = jnp.stack([core_id, local_tile]).astype(jnp.int32)
    grid = (tile_count // GROUP,)
    out_spec = pl.BlockSpec((GROUP, half, row_dev), lambda i, *_: (i, 0, 0))
    flops = 2 * column_count * tile_count * half * rank * row_dev
    mixed_shape = (column_count, rank, row_dev)
    diag_block = (column_count, GROUP, 1, half, rank)

    mixed, given = pl.pallas_call(
        give_kernel,
        grid_spec=pltpu.PrefetchScalarGridSpec(
            num_scalar_prefetch=3,
            grid=grid,
            in_specs=[
                whole(left_factors.shape),
                whole(core.shape),
                pl.BlockSpec(diag_block, lambda i, w, *_: (0, i, 1 - w[0], 0, 0)),
            ],
            out_specs=[whole(mixed_shape), out_spec],
        ),
        out_shape=[
            jax.ShapeDtypeStruct(mixed_shape, jnp.bfloat16),
            jax.ShapeDtypeStruct((tile_count, half, row_dev), jnp.bfloat16),
        ],
        cost_estimate=pl.CostEstimate(flops=flops, bytes_accessed=4 << 20, transcendentals=0),
        compiler_params=pltpu.CompilerParams(vmem_limit_bytes=VMEM_BYTES),
        name="give",
    )(where, tile_ranks, diag_ranks, left_factors, core, diag_rows)
    got = lax.ppermute(given, "panel", swap)
    kept = pl.pallas_call(
        keep_kernel,
        grid_spec=pltpu.PrefetchScalarGridSpec(
            num_scalar_prefetch=1,
            grid=grid,
            in_specs=[
                whole(mixed_shape),
                pl.BlockSpec(diag_block, lambda i, w, *_: (0, i, w[0], 0, 0)),
            ],
            out_specs=out_spec,
        ),
        out_shape=jax.ShapeDtypeStruct((tile_count, half, row_dev), jnp.float32),
        cost_estimate=pl.CostEstimate(flops=flops, bytes_accessed=4 << 20, transcendentals=0),
        compiler_params=pltpu.CompilerParams(vmem_limit_bytes=VMEM_BYTES),
        name="keep",
    )(where, mixed, diag_rows)
    terms = (kept + got.astype(jnp.float32)).astype(jnp.bfloat16)
    parts = lax.all_to_all(
        terms, "panel", split_axis=0, concat_axis=0, tiled=True, axis_index_groups=across
    )
    delta = jnp.sum(parts.astype(jnp.float32), axis=0)
    return target - delta.T


def solution(mesh):
    placed = (
        P("tile", "panel"),
        P("panel", "tile", None),
        P("panel", None, "tile", None),
        P("panel", "tile", None),
        P("panel", "tile", None),
        P("panel", None),
        P("panel"),
    )
    return jax.shard_map(
        shards, mesh=mesh, in_specs=placed, out_specs=P("tile", "panel"), check_vma=False
    )
```

```python
import jax
import jax.numpy as jnp
from jax import lax
from jax.experimental import pallas as pl
from jax.experimental.pallas import tpu as pltpu
from jax.sharding import PartitionSpec as P

CORES = 2
CORE_SCALE = 1024.0
GROUP = 4
VMEM_BYTES = 16 << 20


def mix(where, tranks, dranks, left, core, mixed):
    columns, _, rank = left.shape
    row = lax.broadcasted_iota(jnp.int32, (rank, rank), 0)
    col = lax.broadcasted_iota(jnp.int32, (rank, rank), 1)
    for j in range(columns):
        keep = (row < tranks[j, where[1]]) & (col < dranks[j])
        masked = jnp.where(keep, core[j].astype(jnp.float32), 0.0).astype(jnp.bfloat16)
        mixed[j] = lax.dot_general(
            masked, left[j], (((0,), (1,)), ((), ())), preferred_element_type=jnp.float32
        ).astype(jnp.bfloat16)


def expand(first, diag, mixed, out):
    columns, _, half, rank = diag.shape
    total = None
    for j in range(columns):
        block = diag[j, first : first + GROUP].reshape(GROUP * half, rank)
        part = jnp.dot(block, mixed[j], preferred_element_type=jnp.float32)
        total = part if total is None else total + part
    out[first : first + GROUP] = total.reshape(GROUP, half, -1).astype(out.dtype)


def give_kernel(where, tranks, dranks, left, core, diag, mixed, given, diag_kept, held, arrived, kept):
    tiles = held.shape[1]
    groups = range(0, tiles, GROUP)

    def fetch(n, first):
        part = pl.ds(first, GROUP)
        return pltpu.make_async_copy(
            diag.at[:, part, 1 - where[0]], held.at[:, part], arrived.at[n]
        )

    rest = pltpu.make_async_copy(diag.at[:, :, where[0]], diag_kept, kept)
    for n, first in enumerate(groups):
        fetch(n, first).start()
    rest.start()
    mix(where, tranks, dranks, left, core, mixed)
    for n, first in enumerate(groups):
        fetch(n, first).wait()
        expand(first, held, mixed, given)
    rest.wait()


def keep_kernel(mixed, diag, out):
    for first in range(0, diag.shape[1], GROUP):
        expand(first, diag, mixed, out)


def shards(target, left_factors, right_factors, diag_left, diag_right, tile_ranks, diag_ranks):
    column_count, row_dev, rank = left_factors.shape
    piece = diag_left.shape[1]
    tile_count = lax.axis_size("tile")
    panel_count = lax.axis_size("panel")
    chip_count = panel_count // CORES
    half = piece // CORES
    tile_size = piece * tile_count
    local_tile = lax.axis_index("tile") * row_dev // tile_size
    core_id = lax.axis_index("panel") % CORES
    swap = [(p, p ^ 1) for p in range(panel_count)]
    across = [[CORES * c + a for c in range(chip_count)] for a in range(CORES)]

    diag_rows = lax.all_gather(diag_left, "tile", axis=1, tiled=True)
    diag_rows = diag_rows.reshape(column_count, tile_count, CORES, half, rank)
    diag_rows = pltpu.with_memory_space_constraint(diag_rows, pltpu.HBM)

    partial_product = jnp.einsum(
        "jmcr,jcs->jmrs", right_factors, diag_right, preferred_element_type=jnp.float32
    )
    core_sum = lax.psum((partial_product * CORE_SCALE).astype(jnp.float16), "tile")
    mine = lax.dynamic_index_in_dim(core_sum, local_tile, 1, keepdims=False)
    core = (mine.astype(jnp.float32) * (1.0 / CORE_SCALE)).astype(jnp.bfloat16)

    where = jnp.stack([core_id, local_tile]).astype(jnp.int32)
    flops = 2 * column_count * tile_count * half * rank * row_dev
    cost = pl.CostEstimate(flops=flops, bytes_accessed=4 << 20, transcendentals=0)
    params = pltpu.CompilerParams(vmem_limit_bytes=VMEM_BYTES)
    smem = pl.BlockSpec(memory_space=pltpu.SMEM)
    vmem = pl.BlockSpec(memory_space=pltpu.VMEM)
    diag_half = (column_count, tile_count, half, rank)
    product = (tile_count, half, row_dev)

    mixed, given, diag_kept = pl.pallas_call(
        give_kernel,
        in_specs=[smem, smem, smem, vmem, vmem, pl.BlockSpec(memory_space=pltpu.HBM)],
        out_specs=[vmem, vmem, vmem],
        out_shape=[
            jax.ShapeDtypeStruct((column_count, rank, row_dev), jnp.bfloat16),
            jax.ShapeDtypeStruct(product, jnp.bfloat16),
            jax.ShapeDtypeStruct(diag_half, jnp.bfloat16),
        ],
        scratch_shapes=[
            pltpu.VMEM(diag_half, jnp.bfloat16),
            pltpu.SemaphoreType.DMA((tile_count // GROUP,)),
            pltpu.SemaphoreType.DMA,
        ],
        cost_estimate=cost,
        compiler_params=params,
        name="give",
    )(where, tile_ranks, diag_ranks, left_factors, core, diag_rows)
    got = lax.ppermute(given, "panel", swap)
    kept = pl.pallas_call(
        keep_kernel,
        in_specs=[vmem, vmem],
        out_specs=vmem,
        out_shape=jax.ShapeDtypeStruct(product, jnp.float32),
        cost_estimate=cost,
        compiler_params=params,
        name="keep",
    )(mixed, diag_kept)
    terms = (kept + got.astype(jnp.float32)).astype(jnp.bfloat16)
    parts = lax.all_to_all(
        terms, "panel", split_axis=0, concat_axis=0, tiled=True, axis_index_groups=across
    )
    delta = jnp.sum(parts.astype(jnp.float32), axis=0)
    return target - delta.T


def solution(mesh):
    placed = (
        P("tile", "panel"),
        P("panel", "tile", None),
        P("panel", None, "tile", None),
        P("panel", "tile", None),
        P("panel", "tile", None),
        P("panel", None),
        P("panel"),
    )
    return jax.shard_map(
        shards, mesh=mesh, in_specs=placed, out_specs=P("tile", "panel"), check_vma=False
    )
```

```python
import jax
import jax.numpy as jnp
from jax import lax
from jax.sharding import PartitionSpec as P

CORES = 2
CORE_SCALE = 2.0**10
DIAG_SCALE = 2.0**15


def shards(target, left_factors, right_factors, diag_left, diag_right, tile_ranks, diag_ranks):
    column_count, row_dev, rank = left_factors.shape
    tiles = right_factors.shape[1]
    piece = diag_left.shape[1]
    tile_count = lax.axis_size("tile")
    panel_count = lax.axis_size("panel")
    chip_count = panel_count // CORES
    half = piece // CORES
    columns = CORES * column_count
    tile_size = piece * tile_count
    local_tile = lax.axis_index("tile") * row_dev // tile_size
    first_core = lax.axis_index("panel") % CORES == 0
    swap = [(p, p ^ 1) for p in range(panel_count)]
    to_second = [(CORES * c, CORES * c + 1) for c in range(chip_count)]
    to_first = [(CORES * c + 1, CORES * c) for c in range(chip_count)]
    across = [[CORES * c + a for c in range(chip_count)] for a in range(CORES)]

    positions = jnp.arange(rank)
    right = jnp.where(positions < tile_ranks[:, :, None, None], right_factors, 0)
    diag = jnp.where(positions < diag_ranks[:, None, None], diag_right, 0)

    small = lax.ppermute(jnp.where(first_core, diag, diag_left), "panel", swap)
    large = lax.ppermute(
        jnp.where(first_core, right.reshape(left_factors.shape), left_factors), "panel", swap
    )

    def gather(right, diag, diag_left, small, large):
        both = jnp.concatenate([small, diag_left], 0).reshape(columns, CORES, half, rank)
        both = both.transpose(1, 2, 0, 3).reshape(CORES, half, columns * rank)
        both = (both.astype(jnp.float32) * DIAG_SCALE).astype(jnp.float16)
        rows = lax.all_gather(both, "tile", axis=1, tiled=True)
        return rows, jnp.zeros((columns, rank, rank), jnp.bfloat16)

    def reduce(right, diag, diag_left, small, large):
        right = jnp.concatenate([right, large.reshape(right.shape)], 0)
        diag = jnp.concatenate([diag, small], 0)
        partial_product = jnp.einsum(
            "jmcr,jcs->mjrs", right, diag, preferred_element_type=jnp.float32
        )
        total = lax.psum((partial_product * CORE_SCALE).astype(jnp.float16), "tile")
        mine = lax.dynamic_index_in_dim(total, local_tile, 0, keepdims=False)
        core = (mine.astype(jnp.float32) * (1.0 / CORE_SCALE)).astype(jnp.bfloat16)
        return jnp.zeros((CORES, half * tile_count, columns * rank), jnp.float16), core

    rows, core = lax.cond(
        first_core, gather, reduce, right, diag, diag_left, small, large
    )
    core = lax.ppermute(core, "panel", to_first)
    left = jnp.concatenate([large, left_factors], 0)
    mixed = jnp.einsum("jrs,jnr->jsn", core, left, preferred_element_type=jnp.float32)
    mixed = mixed.astype(jnp.bfloat16).reshape(columns * rank, row_dev)

    def expand(a):
        out = jnp.dot(rows[a].astype(jnp.bfloat16), mixed, preferred_element_type=jnp.float32)
        out = (out * (1.0 / DIAG_SCALE)).astype(jnp.bfloat16)
        return out.reshape(tile_count, half, row_dev)

    got = lax.ppermute(expand(1), "panel", to_second)
    terms = jnp.where(first_core, expand(0), got)
    parts = lax.all_to_all(
        terms, "panel", split_axis=0, concat_axis=0, tiled=True, axis_index_groups=across
    )
    delta = jnp.sum(parts.astype(jnp.float32), axis=0)
    return target - delta.T


def solution(mesh):
    placed = (
        P("tile", "panel"),
        P("panel", "tile", None),
        P("panel", None, "tile", None),
        P("panel", "tile", None),
        P("panel", "tile", None),
        P("panel", None),
        P("panel"),
    )
    return jax.shard_map(
        shards, mesh=mesh, in_specs=placed, out_specs=P("tile", "panel"), check_vma=False
    )
```

```python
import jax
import jax.numpy as jnp
from jax import lax
from jax.experimental import pallas as pl
from jax.experimental.pallas import tpu as pltpu
from jax.sharding import PartitionSpec as P

CORES = 2
CORE_SCALE = 2.0**10
DIAG_SCALE = 2.0**15
VMEM_BYTES = 12 << 20


def mix_kernel(place, tranks, dranks, bundle, ours, mixed):
    columns, row_dev, rank = ours.shape
    cores = CORES * columns
    blocks = row_dev // rank
    row = lax.broadcasted_iota(jnp.int32, (rank, rank), 0)
    col = lax.broadcasted_iota(jnp.int32, (rank, rank), 1)
    for j in range(cores):
        core = bundle[j]
        if j < columns:
            first = cores + blocks * j
            left = bundle[first : first + blocks].reshape(row_dev, rank)
        else:
            mine = j - columns
            keep = (col < tranks[mine, place[0]]) & (row < dranks[mine])
            core = jnp.where(keep, core.astype(jnp.float32), 0.0).astype(core.dtype)
            left = ours[mine]
        part = lax.dot_general(
            core, left, (((1,), (1,)), ((), ())), preferred_element_type=jnp.float32
        )
        mixed[j * rank : (j + 1) * rank] = part.astype(mixed.dtype)


def shards(target, left_factors, right_factors, diag_left, diag_right, tile_ranks, diag_ranks):
    column_count, row_dev, rank = left_factors.shape
    piece = diag_left.shape[1]
    tile_count = lax.axis_size("tile")
    panel_count = lax.axis_size("panel")
    chip_count = panel_count // CORES
    half = piece // CORES
    columns = CORES * column_count
    tile_size = piece * tile_count
    local_tile = lax.axis_index("tile") * row_dev // tile_size
    gathers = lax.axis_index("panel") % CORES == 0
    swap = [(p, p ^ 1) for p in range(panel_count)]
    to_second = [(CORES * c, CORES * c + 1) for c in range(chip_count)]
    to_first = [(CORES * c + 1, CORES * c) for c in range(chip_count)]
    across = [[CORES * c + a for c in range(chip_count)] for a in range(CORES)]

    small = lax.ppermute(jnp.where(gathers, diag_right, diag_left), "panel", swap)
    their_right = lax.ppermute(right_factors, "panel", to_second)

    both = jnp.concatenate([small, diag_left], 0)
    both = both.reshape(columns, CORES, half, rank)
    both = both.transpose(1, 2, 0, 3).reshape(CORES, half, columns * rank)
    both = (both.astype(jnp.float32) * DIAG_SCALE).astype(jnp.float16)

    def reduce(their_right, small):
        positions = jnp.arange(rank)
        kept = positions < diag_ranks[:, None, None]
        right = jnp.where(positions < tile_ranks[:, :, None, None], right_factors, 0)
        right = jnp.concatenate([right, their_right], 0)
        diag = jnp.concatenate([jnp.where(kept, diag_right, 0), small], 0)
        partial_product = jnp.einsum(
            "jmcr,jcs->mjsr", right, diag, preferred_element_type=jnp.float32
        )
        total = lax.psum((partial_product * CORE_SCALE).astype(jnp.float16), "tile")
        mine = lax.dynamic_index_in_dim(total, local_tile, 0, keepdims=False)
        core = (mine.astype(jnp.float32) * (1.0 / CORE_SCALE)).astype(jnp.bfloat16)
        return jnp.concatenate([core, left_factors.reshape(-1, rank, rank)], 0)

    def no_bundle(*_):
        blocks = columns + left_factors.size // (rank * rank)
        return jnp.zeros((blocks, rank, rank), jnp.bfloat16)

    def gather(both):
        rows = lax.all_gather(both, "tile", axis=1, tiled=True)
        return rows, jnp.full((1, 1), 1.0 / DIAG_SCALE, jnp.float32)

    def no_rows(_):
        shape = (CORES, half * tile_count, columns * rank)
        return jnp.zeros(shape, jnp.float16), jnp.zeros((1, 1), jnp.float32)

    bundle = lax.cond(gathers, no_bundle, reduce, their_right, small)
    bundle = lax.ppermute(bundle, "panel", to_first)
    rows, unit = lax.cond(gathers, gather, no_rows, both)

    smem = pl.BlockSpec(memory_space=pltpu.SMEM)
    vmem = pl.BlockSpec(memory_space=pltpu.VMEM)
    mixed = pl.pallas_call(
        mix_kernel,
        in_specs=[smem, smem, smem, vmem, vmem],
        out_specs=vmem,
        out_shape=jax.ShapeDtypeStruct((columns * rank, row_dev), jnp.bfloat16),
        cost_estimate=pl.CostEstimate(
            flops=2 * columns * rank * rank * row_dev, bytes_accessed=4 << 20, transcendentals=0
        ),
        compiler_params=pltpu.CompilerParams(vmem_limit_bytes=VMEM_BYTES),
        name="mix",
    )(local_tile.astype(jnp.int32)[None], tile_ranks, diag_ranks, bundle, left_factors)

    def expand(a):
        out = jnp.dot(rows[a].astype(jnp.bfloat16), mixed, preferred_element_type=jnp.float32)
        out = (out * unit).astype(jnp.bfloat16)
        return out.reshape(tile_count, half, row_dev)

    given = lax.ppermute(expand(1), "panel", to_second)
    terms = jnp.where(gathers, expand(0), given)
    parts = lax.all_to_all(
        terms, "panel", split_axis=0, concat_axis=0, tiled=True, axis_index_groups=across
    )
    delta = jnp.sum(parts.astype(jnp.float32), axis=0)
    return target - delta.T


def solution(mesh):
    placed = (
        P("tile", "panel"),
        P("panel", "tile", None),
        P("panel", None, "tile", None),
        P("panel", "tile", None),
        P("panel", "tile", None),
        P("panel", None),
        P("panel"),
    )
    return jax.shard_map(
        shards, mesh=mesh, in_specs=placed, out_specs=P("tile", "panel"), check_vma=False
    )
```

```python
import jax
import jax.numpy as jnp
from jax import lax
from jax.experimental import pallas as pl
from jax.experimental.pallas import tpu as pltpu
from jax.sharding import PartitionSpec as P

CORES = 2
CORE_SCALE = 2.0**10
DIAG_SCALE = 2.0**15
VMEM_BYTES = 12 << 20


def masked(core, j, place, tranks, dranks):
    row = lax.broadcasted_iota(jnp.int32, core.shape, 0)
    col = lax.broadcasted_iota(jnp.int32, core.shape, 1)
    keep = (col < tranks[j, place[0]]) & (row < dranks[j])
    return jnp.where(keep, core.astype(jnp.float32), 0.0).astype(core.dtype)


def mask_kernel(place, tranks, dranks, cores, left, bundle):
    columns, row_dev, rank = left.shape
    blocks = row_dev // rank
    for j in range(columns):
        bundle[j] = masked(cores[j], j, place, tranks, dranks)
    bundle[columns : CORES * columns] = cores[columns:]
    for j in range(columns):
        first = CORES * columns + j * blocks
        bundle[first : first + blocks] = left[j].reshape(blocks, rank, rank)


def mix_kernel(place, tranks, dranks, bundle, ours, mixed):
    columns, row_dev, rank = ours.shape
    blocks = row_dev // rank
    for j in range(CORES * columns):
        mine = j - columns
        if mine < 0:
            first = CORES * columns + j * blocks
            core, left = bundle[j], bundle[first : first + blocks].reshape(row_dev, rank)
        else:
            core, left = masked(bundle[j], mine, place, tranks, dranks), ours[mine]
        part = lax.dot_general(
            core, left, (((1,), (1,)), ((), ())), preferred_element_type=jnp.float32
        )
        mixed[j * rank : (j + 1) * rank] = part.astype(mixed.dtype)


def shards(target, left_factors, right_factors, diag_left, diag_right, tile_ranks, diag_ranks):
    column_count, row_dev, rank = left_factors.shape
    piece = diag_left.shape[1]
    tile_count = lax.axis_size("tile")
    panel_count = lax.axis_size("panel")
    chip_count = panel_count // CORES
    half = piece // CORES
    columns = CORES * column_count
    tile_size = piece * tile_count
    local_tile = lax.axis_index("tile") * row_dev // tile_size
    gathers = lax.axis_index("panel") % CORES == 0
    swap = [(p, p ^ 1) for p in range(panel_count)]
    to_second = [(CORES * c, CORES * c + 1) for c in range(chip_count)]
    to_first = [(CORES * c + 1, CORES * c) for c in range(chip_count)]
    across = [[CORES * c + a for c in range(chip_count)] for a in range(CORES)]

    small = lax.ppermute(jnp.where(gathers, diag_right, diag_left), "panel", swap)
    their_right = lax.ppermute(right_factors, "panel", to_second)

    both = jnp.concatenate([small, diag_left], 0)
    both = both.reshape(columns, CORES, half, rank)
    both = both.transpose(1, 2, 0, 3).reshape(CORES, half, columns * rank)
    both = (both.astype(jnp.float32) * DIAG_SCALE).astype(jnp.float16)

    place = local_tile.astype(jnp.int32)[None]
    smem = pl.BlockSpec(memory_space=pltpu.SMEM)
    vmem = pl.BlockSpec(memory_space=pltpu.VMEM)
    params = pltpu.CompilerParams(vmem_limit_bytes=VMEM_BYTES)

    bundled = (columns + left_factors.size // (rank * rank), rank, rank)

    def reduce(their_right, small):
        right = jnp.concatenate([right_factors, their_right], 0)
        diag = jnp.concatenate([diag_right, small], 0)
        partial_product = jnp.einsum(
            "jmcr,jcs->mjsr", right, diag, preferred_element_type=jnp.float32
        )
        total = lax.psum((partial_product * CORE_SCALE).astype(jnp.float16), "tile")
        mine = lax.dynamic_index_in_dim(total, local_tile, 0, keepdims=False)
        mine = (mine.astype(jnp.float32) * (1.0 / CORE_SCALE)).astype(jnp.bfloat16)
        return pl.pallas_call(
            mask_kernel,
            in_specs=[smem, smem, smem, vmem, vmem],
            out_specs=vmem,
            out_shape=jax.ShapeDtypeStruct(bundled, mine.dtype),
            compiler_params=params,
            name="mask",
        )(place, tile_ranks, diag_ranks, mine, left_factors)

    def no_bundle(*_):
        return jnp.zeros(bundled, jnp.bfloat16)

    def gather(both):
        rows = lax.all_gather(both, "tile", axis=1, tiled=True)
        return rows, jnp.full((1, 1), 1.0 / DIAG_SCALE, jnp.float32)

    def no_rows(_):
        shape = (CORES, half * tile_count, columns * rank)
        return jnp.zeros(shape, jnp.float16), jnp.zeros((1, 1), jnp.float32)

    bundle = lax.cond(gathers, no_bundle, reduce, their_right, small)
    bundle = lax.ppermute(bundle, "panel", to_first)
    rows, unit = lax.cond(gathers, gather, no_rows, both)

    mixed = pl.pallas_call(
        mix_kernel,
        in_specs=[smem, smem, smem, vmem, vmem],
        out_specs=vmem,
        out_shape=jax.ShapeDtypeStruct((columns * rank, row_dev), jnp.bfloat16),
        cost_estimate=pl.CostEstimate(
            flops=2 * columns * rank * rank * row_dev, bytes_accessed=4 << 20, transcendentals=0
        ),
        compiler_params=params,
        name="mix",
    )(place, tile_ranks, diag_ranks, bundle, left_factors)

    def expand(a):
        out = jnp.dot(rows[a].astype(jnp.bfloat16), mixed, preferred_element_type=jnp.float32)
        out = (out * unit).astype(jnp.bfloat16)
        return out.reshape(tile_count, half, row_dev)

    given = lax.ppermute(expand(1), "panel", to_second)
    terms = jnp.where(gathers, expand(0), given)
    parts = lax.all_to_all(
        terms, "panel", split_axis=0, concat_axis=0, tiled=True, axis_index_groups=across
    )
    delta = jnp.sum(parts.astype(jnp.float32), axis=0)
    return target - delta.T


def solution(mesh):
    placed = (
        P("tile", "panel"),
        P("panel", "tile", None),
        P("panel", None, "tile", None),
        P("panel", "tile", None),
        P("panel", "tile", None),
        P("panel", None),
        P("panel"),
    )
    return jax.shard_map(
        shards, mesh=mesh, in_specs=placed, out_specs=P("tile", "panel"), check_vma=False
    )
```

```python
import jax
import jax.numpy as jnp
from jax import lax
from jax.experimental import pallas as pl
from jax.experimental.pallas import tpu as pltpu
from jax.sharding import PartitionSpec as P

CORES = 2
CORE_SCALE = 2.0**10
DIAG_SCALE = 2.0**15
VMEM_BYTES = 12 << 20


def masked(core, j, place, tranks, dranks):
    row = lax.broadcasted_iota(jnp.int32, core.shape, 0)
    col = lax.broadcasted_iota(jnp.int32, core.shape, 1)
    keep = (col < tranks[j, place[0]]) & (row < dranks[j])
    return jnp.where(keep, core.astype(jnp.float32), 0.0).astype(core.dtype)


def mask_kernel(place, tranks, dranks, cores, left, bundle):
    columns, row_dev, rank = left.shape
    blocks = row_dev // rank
    for j in range(columns):
        bundle[j] = masked(cores[j], j, place, tranks, dranks)
    bundle[columns : CORES * columns] = cores[columns:]
    for j in range(columns):
        first = CORES * columns + j * blocks
        bundle[first : first + blocks] = left[j].reshape(blocks, rank, rank)


def mix_kernel(place, tranks, dranks, bundle, ours, mixed):
    columns, row_dev, rank = ours.shape
    blocks = row_dev // rank
    for j in range(CORES * columns):
        mine = j - columns
        if mine < 0:
            first = CORES * columns + j * blocks
            core, left = bundle[j], bundle[first : first + blocks].reshape(row_dev, rank)
        else:
            core, left = masked(bundle[j], mine, place, tranks, dranks), ours[mine]
        part = lax.dot_general(
            core, left, (((1,), (1,)), ((), ())), preferred_element_type=jnp.float32
        )
        mixed[j * rank : (j + 1) * rank] = part.astype(mixed.dtype)


def shards(target, left_factors, right_factors, diag_left, diag_right, tile_ranks, diag_ranks):
    column_count, row_dev, rank = left_factors.shape
    piece = diag_left.shape[1]
    tile_count = lax.axis_size("tile")
    panel_count = lax.axis_size("panel")
    chip_count = panel_count // CORES
    half = piece // CORES
    columns = CORES * column_count
    tile_size = piece * tile_count
    local_tile = lax.axis_index("tile") * row_dev // tile_size
    gathers = lax.axis_index("panel") % CORES == 0
    swap = [(p, p ^ 1) for p in range(panel_count)]
    to_second = [(CORES * c, CORES * c + 1) for c in range(chip_count)]
    to_first = [(CORES * c + 1, CORES * c) for c in range(chip_count)]
    across = [[CORES * c + a for c in range(chip_count)] for a in range(CORES)]

    small = lax.ppermute(jnp.where(gathers, diag_right, diag_left), "panel", swap)
    their_right = lax.ppermute(right_factors, "panel", to_second)

    both = jnp.concatenate([small, diag_left], 0)
    both = both.reshape(columns, CORES, half, rank)
    both = both.transpose(1, 2, 0, 3).reshape(CORES, half, columns * rank)
    both = (both.astype(jnp.float32) * DIAG_SCALE).astype(jnp.float16)

    place = local_tile.astype(jnp.int32)[None]
    smem = pl.BlockSpec(memory_space=pltpu.SMEM)
    vmem = pl.BlockSpec(memory_space=pltpu.VMEM)
    params = pltpu.CompilerParams(vmem_limit_bytes=VMEM_BYTES)

    bundled = (columns + left_factors.size // (rank * rank), rank, rank)

    def reduce(their_right, small):
        right = jnp.concatenate([right_factors, their_right], 0)
        diag = jnp.concatenate([diag_right, small], 0)
        partial_product = jnp.einsum(
            "jmcr,jcs->mjsr", right, diag, preferred_element_type=jnp.float32
        )
        total = lax.psum((partial_product * CORE_SCALE).astype(jnp.float16), "tile")
        mine = lax.dynamic_index_in_dim(total, local_tile, 0, keepdims=False)
        mine = (mine.astype(jnp.float32) * (1.0 / CORE_SCALE)).astype(jnp.bfloat16)
        return pl.pallas_call(
            mask_kernel,
            in_specs=[smem, smem, smem, vmem, vmem],
            out_specs=vmem,
            out_shape=jax.ShapeDtypeStruct(bundled, mine.dtype),
            compiler_params=params,
            name="mask",
        )(place, tile_ranks, diag_ranks, mine, left_factors)

    def no_bundle(*_):
        return jnp.zeros(bundled, jnp.bfloat16)

    def gather(both):
        rows = lax.all_gather(both, "tile", axis=1, tiled=True)
        return rows, jnp.full((1, 1), 1.0 / DIAG_SCALE, jnp.float32)

    def no_rows(_):
        shape = (CORES, half * tile_count, columns * rank)
        return jnp.zeros(shape, jnp.float16), jnp.zeros((1, 1), jnp.float32)

    bundle = lax.cond(gathers, no_bundle, reduce, their_right, small)
    bundle = lax.ppermute(bundle, "panel", to_first)
    rows, unit = lax.cond(gathers, gather, no_rows, both)

    mixed = pl.pallas_call(
        mix_kernel,
        in_specs=[smem, smem, smem, vmem, vmem],
        out_specs=vmem,
        out_shape=jax.ShapeDtypeStruct((columns * rank, row_dev), jnp.bfloat16),
        cost_estimate=pl.CostEstimate(
            flops=2 * columns * rank * rank * row_dev, bytes_accessed=4 << 20, transcendentals=0
        ),
        compiler_params=params,
        name="mix",
    )(place, tile_ranks, diag_ranks, bundle, left_factors)

    def expand(a):
        out = jnp.dot(rows[a].astype(jnp.bfloat16), mixed, preferred_element_type=jnp.float32)
        out = (out * unit).astype(jnp.bfloat16)
        return out.reshape(tile_count, half, row_dev)

    given = lax.ppermute(expand(1), "panel", to_second)
    terms = jnp.where(gathers, expand(0), given)
    parts = lax.all_to_all(
        terms, "panel", split_axis=0, concat_axis=0, tiled=True, axis_index_groups=across
    )
    rest = target.T
    for part in range(chip_count):
        rest = rest - parts[part].astype(jnp.float32)
    return rest.T


def solution(mesh):
    placed = (
        P("tile", "panel"),
        P("panel", "tile", None),
        P("panel", None, "tile", None),
        P("panel", "tile", None),
        P("panel", "tile", None),
        P("panel", None),
        P("panel"),
    )
    return jax.shard_map(
        shards, mesh=mesh, in_specs=placed, out_specs=P("tile", "panel"), check_vma=False
    )
```

```python
import jax
import jax.numpy as jnp
from jax import lax
from jax.experimental import pallas as pl
from jax.experimental.pallas import tpu as pltpu
from jax.sharding import PartitionSpec as P

CORES = 2
CORE_SCALE = 2.0**10
DIAG_SCALE = 2.0**15
VMEM_BYTES = 7 << 20


def masked(core, j, place, tranks, dranks):
    row = lax.broadcasted_iota(jnp.int32, core.shape, 0)
    col = lax.broadcasted_iota(jnp.int32, core.shape, 1)
    keep = (col < tranks[j, place[0]]) & (row < dranks[j])
    return jnp.where(keep, core.astype(jnp.float32), 0.0).astype(core.dtype)


def mask_kernel(place, tranks, dranks, cores, left, bundle):
    columns, row_dev, rank = left.shape
    blocks = row_dev // rank
    for j in range(columns):
        bundle[j] = masked(cores[j], j, place, tranks, dranks)
    bundle[columns : CORES * columns] = cores[columns:]
    for j in range(columns):
        first = CORES * columns + j * blocks
        bundle[first : first + blocks] = left[j].reshape(blocks, rank, rank)


def mix_kernel(place, tranks, dranks, bundle, ours, mixed):
    columns, row_dev, rank = ours.shape
    blocks = row_dev // rank
    for j in range(CORES * columns):
        mine = j - columns
        if mine < 0:
            first = CORES * columns + j * blocks
            core, left = bundle[j], bundle[first : first + blocks].reshape(row_dev, rank)
        else:
            core, left = masked(bundle[j], mine, place, tranks, dranks), ours[mine]
        part = lax.dot_general(
            core, left, (((1,), (1,)), ((), ())), preferred_element_type=jnp.float32
        )
        mixed[j * rank : (j + 1) * rank] = part.astype(mixed.dtype)


def shards(target, left_factors, right_factors, diag_left, diag_right, tile_ranks, diag_ranks):
    column_count, row_dev, rank = left_factors.shape
    piece = diag_left.shape[1]
    tile_count = lax.axis_size("tile")
    panel_count = lax.axis_size("panel")
    chip_count = panel_count // CORES
    half = piece // CORES
    columns = CORES * column_count
    tile_size = piece * tile_count
    local_tile = lax.axis_index("tile") * row_dev // tile_size
    gathers = lax.axis_index("panel") % CORES == 0
    swap = [(p, p ^ 1) for p in range(panel_count)]
    to_second = [(CORES * c, CORES * c + 1) for c in range(chip_count)]
    to_first = [(CORES * c + 1, CORES * c) for c in range(chip_count)]
    across = [[CORES * c + a for c in range(chip_count)] for a in range(CORES)]

    small = lax.ppermute(jnp.where(gathers, diag_right, diag_left), "panel", swap)
    their_right = lax.ppermute(right_factors, "panel", to_second)

    both = jnp.concatenate([small, diag_left], 0)
    both = both.reshape(columns, CORES, half, rank)
    both = both.transpose(1, 2, 0, 3).reshape(CORES, half, columns * rank)
    both = (both.astype(jnp.float32) * DIAG_SCALE).astype(jnp.float16)

    place = local_tile.astype(jnp.int32)[None]
    smem = pl.BlockSpec(memory_space=pltpu.SMEM)
    vmem = pl.BlockSpec(memory_space=pltpu.VMEM)
    params = pltpu.CompilerParams(vmem_limit_bytes=VMEM_BYTES)

    bundled = (columns + left_factors.size // (rank * rank), rank, rank)

    def reduce(their_right, small):
        right = jnp.concatenate([right_factors, their_right], 0)
        diag = jnp.concatenate([diag_right, small], 0)
        partial_product = jnp.einsum(
            "jmcr,jcs->mjsr", right, diag, preferred_element_type=jnp.float32
        )
        total = lax.psum((partial_product * CORE_SCALE).astype(jnp.float16), "tile")
        mine = lax.dynamic_index_in_dim(total, local_tile, 0, keepdims=False)
        mine = (mine.astype(jnp.float32) * (1.0 / CORE_SCALE)).astype(jnp.bfloat16)
        return pl.pallas_call(
            mask_kernel,
            in_specs=[smem, smem, smem, vmem, vmem],
            out_specs=vmem,
            out_shape=jax.ShapeDtypeStruct(bundled, mine.dtype),
            compiler_params=params,
            name="mask",
        )(place, tile_ranks, diag_ranks, mine, left_factors)

    def no_bundle(*_):
        return jnp.zeros(bundled, jnp.bfloat16)

    def gather(both):
        rows = lax.all_gather(both, "tile", axis=1, tiled=True)
        return rows, jnp.full((1, 1), 1.0 / DIAG_SCALE, jnp.float32)

    def no_rows(_):
        shape = (CORES, half * tile_count, columns * rank)
        return jnp.zeros(shape, jnp.float16), jnp.zeros((1, 1), jnp.float32)

    bundle = lax.cond(gathers, no_bundle, reduce, their_right, small)
    bundle = lax.ppermute(bundle, "panel", to_first)
    rows, unit = lax.cond(gathers, gather, no_rows, both)

    mixed = pl.pallas_call(
        mix_kernel,
        in_specs=[smem, smem, smem, vmem, vmem],
        out_specs=vmem,
        out_shape=jax.ShapeDtypeStruct((columns * rank, row_dev), jnp.bfloat16),
        cost_estimate=pl.CostEstimate(
            flops=2 * columns * rank * rank * row_dev, bytes_accessed=4 << 20, transcendentals=0
        ),
        compiler_params=params,
        name="mix",
    )(place, tile_ranks, diag_ranks, bundle, left_factors)

    def expand(a):
        out = jnp.dot(rows[a].astype(jnp.bfloat16), mixed, preferred_element_type=jnp.float32)
        out = (out * unit).astype(jnp.bfloat16)
        return out.reshape(tile_count, half, row_dev)

    given = lax.ppermute(expand(1), "panel", to_second)
    terms = jnp.where(gathers, expand(0), given)
    parts = lax.all_to_all(
        terms, "panel", split_axis=0, concat_axis=0, tiled=True, axis_index_groups=across
    )
    rest = target.T
    for part in range(chip_count):
        rest = rest - parts[part].astype(jnp.float32)
    return rest.T


def solution(mesh):
    placed = (
        P("tile", "panel"),
        P("panel", "tile", None),
        P("panel", None, "tile", None),
        P("panel", "tile", None),
        P("panel", "tile", None),
        P("panel", None),
        P("panel"),
    )
    return jax.shard_map(
        shards, mesh=mesh, in_specs=placed, out_specs=P("tile", "panel"), check_vma=False
    )
```
